32 devices in a mesh: freq: 4 (over y, x), rcv: 8 (over z, core).
Axes of the slice: x: 2, y: 2, z: 4, core: 2. Of those that a mesh axis runs over, the one named last changes fastest.
Arguments:
- up_time: bfloat16 [32, 256, 20480], P(('freq', 'rcv')), may hold values from -74 to 74
- down_blocks: bfloat16 [8, 160, 11, 2, 128, 128], P('freq', 'rcv'), may hold values from -0.09375 to 0.09375
- block_cols: int32 [8, 160, 11], P('freq', 'rcv'), may hold values from 0 to 159, as said below
- block_counts: int32 [8, 160], P('freq', 'rcv'), may hold values from 1 to 11, as said below
Outputs:
- solution: float32 [2, 8, 32, 20480], P(None, 'freq', None, 'rcv')
- normal_residual: float32 [2, 8, 32, 20480], P(None, 'freq', None, 'rcv')
The draws below stay inside these ranges and needn't reach their ends.
Inputs may be any that keep to these rules, and one draw needn't show every extreme that they name: block_cols[f, r, s] is the column block of slot s of row block r at frequency f; it differs from r by at most 5. Row block r of frequency f stores blocks in its first block_counts[f, r] slots.
All inputs are finite; a program needn't handle non-finite values.
Results may differ from the reference program's by a relative error of at most 0.0062.
Values may be sent and summed in bfloat16 or wider, within the bound.
A program may use at most 192 MiB of HBM per device.

```python
import math
import jax
import jax.numpy as jnp
from jax import lax

NR = 20480
BLK = 128
REACH = 5
NT = 256
ITERS = 2
SLOTS = 11
NB = 160
NV = 32
NF = 8


def draw_up_time(key, part):
    folded = jax.random.fold_in(key, 37)
    key_traces, key_rough, key_shots = jax.random.split(folded, 3)
    receiver = jnp.arange(NR, dtype=jnp.float32)
    receiver_ramp = jnp.sqrt(1.0 + 2.0 * receiver / NR)[None, None, :]
    roughness = jnp.exp(jax.random.uniform(key_rough, (1, 1, NR), jnp.float32, -1.15, 1.15))
    shot_gain = jnp.exp(jax.random.uniform(key_shots, (NV, 1, 1), jnp.float32, -0.8, 0.8))
    traces = jax.random.normal(key_traces, (NV, NT, NR), jnp.float32)
    traces = jnp.clip(traces, -6.0, 6.0)
    return (traces * receiver_ramp * roughness * shot_gain).astype(jnp.bfloat16)


def draw_block_cols(key, part):
    folded = jax.random.fold_in(key, 23)
    scores = jax.random.randint(folded, (NF, NB, SLOTS), 0, 1 << 20) * SLOTS + jnp.arange(SLOTS, dtype=jnp.int32)
    ranking = jnp.argsort(scores, axis=-1).astype(jnp.int32)
    offsets = ranking - REACH
    row_ids = jnp.arange(NB, dtype=jnp.int32)[None, :, None]
    columns = row_ids + offsets
    columns = jnp.where((columns < 0) | (columns >= NB), row_ids - offsets, columns)
    return columns.astype(jnp.int32)


def draw_block_counts(key, part):
    folded = jax.random.fold_in(key, 11)
    key_one, key_two, key_full, key_single = jax.random.split(folded, 4)
    random_one = jax.random.randint(key_one, (NF, NB), 0, SLOTS)
    random_two = jax.random.randint(key_two, (NF, NB), 0, SLOTS)
    divisor = max(1, (SLOTS - 1) // 2)
    counts = jnp.minimum(SLOTS, 1 + random_one * random_two // divisor)
    full_row = jax.random.randint(key_full, (NF, 1), 0, NB)
    single_row = (full_row + 1 + jax.random.randint(key_single, (NF, 1), 0, NB - 1)) % NB
    row_ids = jnp.arange(NB, dtype=jnp.int32)[None, :]
    counts = jnp.where(row_ids == full_row, SLOTS, counts)
    counts = jnp.where(row_ids == single_row, 1, counts)
    return counts.astype(jnp.int32)


def level_of(own_key, shape, cuts, least, high):
    loudness, own = 1.0, jax.random.fold_in(own_key, 6)
    for position, parts in cuts:
        steps = jnp.exp(jax.random.uniform(jax.random.fold_in(own, position), (parts,), jnp.float32, least / len(cuts), high / len(cuts)))
        loudness = loudness * jnp.repeat(steps, shape[position] // parts).reshape([-1 if axis == position else 1 for axis in range(len(shape))])
    return loudness


def scatter_about(own_key, dims, spread, limit, pieces=(), kind=jnp.bfloat16):
    loudness = level_of(own_key, dims, pieces, -0.22, 0.18) if pieces else 1.0
    drawn = jax.random.normal(own_key, dims, jnp.float32) * spread * loudness
    return jnp.minimum(jnp.maximum(drawn, -limit), limit).astype(kind)


def setup_inputs(seed: int = 0) -> dict:
    splits = jax.random.split(jax.random.key(seed), 5)
    up_time = draw_up_time(jax.random.fold_in(splits[4], 71), 0)
    down_blocks = scatter_about(splits[1], (NF, NB, SLOTS, 2, BLK, BLK), (3 * BLK * SLOTS) ** -0.5, 0.09375, ((0, 4), (1, 8)))
    block_cols = draw_block_cols(jax.random.fold_in(splits[4], 71), 0)
    block_counts = draw_block_counts(jax.random.fold_in(splits[4], 71), 0)
    return {"up_time": up_time, "down_blocks": down_blocks, "block_cols": block_cols, "block_counts": block_counts}


EPSILON = 1e-06

def fourier_table(time_steps, freq_groups, local_freqs):
    shape = (time_steps, freq_groups, local_freqs)
    sample = lax.broadcasted_iota(jnp.int32, shape, 0)
    harmonic = lax.broadcasted_iota(jnp.int32, shape, 1) * local_freqs + lax.broadcasted_iota(jnp.int32, shape, 2) + 1
    phase_angle = 2.0 * math.pi / time_steps * (harmonic * sample % time_steps).astype(jnp.float32)
    scale_factor = 1.0 / math.sqrt(time_steps)
    return jnp.stack([jnp.cos(phase_angle) * scale_factor, -jnp.sin(phase_angle) * scale_factor], axis=1).astype(jnp.bfloat16)

def field_norm(field):
    return jnp.sqrt(jnp.sum(field * field) + EPSILON)

def rounded_field(field):
    return lax.optimization_barrier(field.astype(jnp.bfloat16)).astype(jnp.float32).reshape(2, NV, NB, BLK)

def live_mask(counts):
    return (lax.broadcasted_iota(jnp.int32, (NB, SLOTS), 1) < counts[:, None]).astype(jnp.float32)

def forward(field, blocks, columns, counts):
    rounded = rounded_field(field)
    gathered = rounded[:, :, columns, :] * live_mask(counts)[None, None, :, :, None]
    products = jnp.einsum('cvrsj,rseij->cevri', gathered, blocks.astype(jnp.float32))
    real_part = products[0, 0] - products[1, 1]
    imaginary = products[0, 1] + products[1, 0]
    return field + jnp.stack([real_part, imaginary]).reshape(2, NV, NR)

def adjoint(field, blocks, columns, counts):
    rounded = rounded_field(field)
    products = jnp.einsum('cvri,rseij->cevrsj', rounded, blocks.astype(jnp.float32))
    contributions = jnp.stack([products[0, 0] + products[1, 1], products[1, 0] - products[0, 1]])
    contributions = contributions * live_mask(counts)[None, None, :, :, None]
    summed = jnp.zeros((2, NV, NB, BLK), jnp.float32).at[:, :, columns.reshape(-1), :].add(contributions.reshape(2, NV, NB * SLOTS, BLK))
    return field + summed.reshape(2, NV, NR)

def solve_frequency(inputs):
    right_side, blocks, columns, counts = inputs
    beta_norm = field_norm(right_side)
    left_vector = right_side / beta_norm
    residual_right = adjoint(left_vector, blocks, columns, counts)
    alpha_norm = field_norm(residual_right)
    right_vector = residual_right / alpha_norm
    search_direction = right_vector
    solution = jnp.zeros_like(right_side)
    phibar = beta_norm
    rhobar = alpha_norm
    for iteration in range(ITERS):
        residual_left = forward(right_vector, blocks, columns, counts) - alpha_norm * left_vector
        beta_norm = field_norm(residual_left)
        left_vector = residual_left / beta_norm
        residual_right = adjoint(left_vector, blocks, columns, counts) - beta_norm * right_vector
        alpha_norm = field_norm(residual_right)
        right_vector = residual_right / alpha_norm
        rho_value = jnp.sqrt(rhobar * rhobar + beta_norm * beta_norm)
        cosine = rhobar / rho_value
        sine_value = beta_norm / rho_value
        theta_value = sine_value * alpha_norm
        rhobar = -cosine * alpha_norm
        phi_value = cosine * phibar
        phibar = sine_value * phibar
        solution = solution + phi_value / rho_value * search_direction
        search_direction = right_vector - theta_value / rho_value * search_direction
    return (solution, phibar * alpha_norm * cosine * right_vector)

def reference(up_time, down_blocks, block_cols, block_counts):
    transposed = fourier_table(NT, 1, NF).reshape(NT, 2 * NF).T

    def one_shot(shot_trace):
        return jnp.dot(transposed, shot_trace, preferred_element_type=jnp.float32)
    spectra = lax.map(one_shot, up_time)
    spectra = lax.optimization_barrier(spectra.astype(jnp.bfloat16)).astype(jnp.float32)
    right_side = spectra.reshape(NV, 2, NF, NR).transpose(2, 1, 0, 3)
    solutions, residuals = lax.map(solve_frequency, (right_side, down_blocks, block_cols, block_counts))
    return (solutions.transpose(1, 0, 2, 3), residuals.transpose(1, 0, 2, 3))
```

```python
import functools
import math

import jax
import jax.numpy as jnp
from jax import lax
from jax.experimental import pallas as pl
from jax.experimental.pallas import tpu as pltpu
from jax.sharding import PartitionSpec as P

ITERS = 2
EPSILON = 1e-06
GROUP = 4


def fourier_table(time_steps, freqs):
    shape = (time_steps, freqs)
    sample = lax.broadcasted_iota(jnp.int32, shape, 0)
    harmonic = lax.broadcasted_iota(jnp.int32, shape, 1) + 1
    phase_angle = 2.0 * math.pi / time_steps * (harmonic * sample % time_steps).astype(jnp.float32)
    scale_factor = 1.0 / math.sqrt(time_steps)
    return jnp.stack(
        [jnp.cos(phase_angle) * scale_factor, -jnp.sin(phase_angle) * scale_factor], axis=1
    ).astype(jnp.bfloat16)


def pass_kernel(first, dims, *refs):
    freqs, rows, slots, blk, reach, sources = dims
    if first:
        counts, cols, blocks, start, t, psq, buf, lhs, item_row, item_f, item_a, item_b, item_buf, sems = refs
    else:
        (counts, cols, scale, blocks, field, prev, p_out, t, psq,
         buf, lhs, item_row, item_f, item_a, item_b, item_buf, sems, zb, acc) = refs
    span = rows + 2 * reach
    pairs = (slots + 1) // 2
    total_rows = freqs * rows
    base = lax.axis_index("rcv") * rows - reach

    def lanes(index):
        return pl.ds(pl.multiple_of(index * blk, blk), blk)

    def copy_of(f, r, s0, item):
        return pltpu.make_async_copy(
            blocks.at[f, r, pl.ds(s0, 2)], buf.at[item], sems.at[item // GROUP]
        )

    total = jnp.int32(0)
    for f in range(freqs):
        def each_row(r, n, f=f):
            fr = f * rows + r
            count = counts[fr]
            here = (count + 1) // 2

            def each_pair(k, carry):
                item = n + k
                s0 = jnp.minimum(2 * k, slots - 2)
                copy_of(f, r, s0, item).start()
                item_row[item] = fr
                item_f[item] = f
                item_buf[item] = item
                item_a[item] = jnp.where(s0 == 2 * k, cols[fr * slots + s0] - base, span)
                item_b[item] = jnp.where(s0 + 1 < count, cols[fr * slots + s0 + 1] - base, span)
                return carry

            lax.fori_loop(0, here, each_pair, 0)
            return n + here

        total = lax.fori_loop(0, rows, each_row, total)
    for j in range(GROUP):
        item_row[total + j] = total_rows
        item_f[total + j] = 0
        item_buf[total + j] = 0
        item_a[total + j] = span
        item_b[total + j] = span
    groups = (total + GROUP - 1) // GROUP

    def arrive(g):
        for j in range(GROUP):
            @pl.when(g * GROUP + j < total)
            def _():
                copy_of(0, 0, 0, g * GROUP + j).wait()

    t[...] = jnp.zeros_like(t)
    lhs[total_rows] = jnp.zeros(lhs.shape[1:], lhs.dtype)
    if not first:
        zb[:, :, :, : span * blk] = field[...].astype(jnp.bfloat16)
        zb[:, :, :, span * blk :] = jnp.zeros((2, freqs, sources, blk), jnp.bfloat16)
        acc[...] = jnp.zeros_like(acc)

        def forward(g, carry):
            arrive(g)
            for j in range(GROUP):
                i = g * GROUP + j
                f = item_f[i]
                za = zb[:, f, :, lanes(item_a[i])].reshape(2 * sources, blk)
                zc = zb[:, f, :, lanes(item_b[i])].reshape(2 * sources, blk)
                weights = buf[item_buf[i]].reshape(2, 2 * blk, blk)
                out = lax.dot_general(
                    jnp.concatenate([za, zc], axis=1),
                    jnp.concatenate([weights[0], weights[1]], axis=1),
                    (((1,), (1,)), ((), ())),
                    preferred_element_type=jnp.float32,
                )
                acc[item_row[i]] += out
            return carry

        lax.fori_loop(0, groups, forward, 0)

    for f in range(freqs):
        def finish(r, sums, f=f):
            fr = f * rows + r
            if first:
                real = start[0, f, :, lanes(r)]
                imag = start[1, f, :, lanes(r)]
                real16, imag16 = real, imag
                real, imag = real.astype(jnp.float32), imag.astype(jnp.float32)
            else:
                a = acc[fr]
                real = (
                    field[0, f, :, lanes(r + reach)]
                    + (a[:sources, :blk] - a[sources:, blk:])
                    - scale[f] * prev[0, f, :, lanes(r)]
                )
                imag = (
                    field[1, f, :, lanes(r + reach)]
                    + (a[:sources, blk:] + a[sources:, :blk])
                    - scale[f] * prev[1, f, :, lanes(r)]
                )
                p_out[0, f, :, lanes(r)] = real
                p_out[1, f, :, lanes(r)] = imag
                real16, imag16 = real.astype(jnp.bfloat16), imag.astype(jnp.bfloat16)
            t[0, f, :, lanes(r + reach)] = real
            t[1, f, :, lanes(r + reach)] = imag
            lhs[fr, :sources, :blk] = real16
            lhs[fr, :sources, blk:] = imag16
            lhs[fr, sources:, :blk] = imag16
            lhs[fr, sources:, blk:] = -real16
            squares = real * real + imag * imag
            return sums + jnp.sum(squares.reshape(sources // 8, 8, blk), axis=0)

        psq[f] = lax.fori_loop(0, rows, finish, jnp.zeros((8, blk), jnp.float32))

    def adjoint(g, carry):
        if first:
            arrive(g)
        for j in range(GROUP):
            i = g * GROUP + j
            f = item_f[i]
            weights = buf[item_buf[i]].reshape(2, 2 * blk, blk)
            out = jnp.dot(
                lhs[item_row[i]],
                jnp.concatenate([weights[0], weights[1]], axis=1),
                preferred_element_type=jnp.float32,
            )
            for index, half in ((item_a[i], out[:, :blk]), (item_b[i], out[:, blk:])):
                t[:, f, :, lanes(index)] += half.reshape(2, sources, blk)
        return carry

    lax.fori_loop(0, groups, adjoint, 0)


def operator_pass(counts, cols, blocks, start=None, field=None, prev=None, scale=None):
    freqs, rows, slots, _, blk, _ = blocks.shape
    first = start is not None
    sources = (start if first else prev).shape[2]
    reach = (slots - 1) // 2
    span = rows + 2 * reach
    pairs = (slots + 1) // 2
    items = freqs * rows * pairs
    dims = (freqs, rows, slots, blk, reach, sources)
    smem = pl.BlockSpec(memory_space=pltpu.SMEM)
    vmem = pl.BlockSpec(memory_space=pltpu.VMEM)
    hbm = pl.BlockSpec(memory_space=pl.ANY)
    t_shape = jax.ShapeDtypeStruct((2, freqs, sources, (span + 1) * blk), jnp.float32)
    psq_shape = jax.ShapeDtypeStruct((freqs, 8, blk), jnp.float32)
    listed = (items + GROUP,)
    scratch = [
        pltpu.VMEM((items, 2, 2, blk, blk), jnp.bfloat16),
        pltpu.VMEM((freqs * rows + 1, 2 * sources, 2 * blk), jnp.bfloat16),
        pltpu.SMEM(listed, jnp.int32),
        pltpu.SMEM(listed, jnp.int32),
        pltpu.SMEM(listed, jnp.int32),
        pltpu.SMEM(listed, jnp.int32),
        pltpu.SMEM(listed, jnp.int32),
        pltpu.SemaphoreType.DMA(((items + GROUP - 1) // GROUP,)),
    ]
    if first:
        args = (counts, cols, blocks, start)
        in_specs = [smem, smem, hbm, vmem]
        out_shape = (t_shape, psq_shape)
    else:
        args = (counts, cols, scale, blocks, field, prev)
        in_specs = [smem, smem, smem, hbm, vmem, vmem]
        out_shape = (jax.ShapeDtypeStruct(prev.shape, jnp.float32), t_shape, psq_shape)
        scratch += [
            pltpu.VMEM((2, freqs, sources, (span + 1) * blk), jnp.bfloat16),
            pltpu.VMEM((freqs * rows + 1, 2 * sources, 2 * blk), jnp.float32),
        ]
    return pl.pallas_call(
        functools.partial(pass_kernel, first, dims),
        out_shape=out_shape,
        in_specs=in_specs,
        out_specs=tuple(vmem for _ in out_shape),
        scratch_shapes=scratch,
        compiler_params=pltpu.CompilerParams(vmem_limit_bytes=56 * 1024 * 1024),
        name="first_adjoint" if first else "forward_adjoint",
    )(*args)


def body(up_time, down_blocks, block_cols, block_counts):
    freq_groups = lax.axis_size("freq")
    receiver_groups = lax.axis_size("rcv")
    shot_count, time_steps, receivers = up_time.shape
    local_freqs, local_blocks, slot_count, _, block_size, _ = down_blocks.shape
    local_rows = receivers // receiver_groups
    reach_blocks = (slot_count - 1) // 2
    rim = reach_blocks * block_size
    fourier = fourier_table(time_steps, freq_groups * local_freqs)
    fourier = fourier.reshape(time_steps, -1).T
    spectrum = jnp.stack(
        [
            jnp.dot(fourier, up_time[s], preferred_element_type=jnp.float32).astype(jnp.bfloat16)
            for s in range(shot_count)
        ],
        axis=1,
    )
    spectrum = spectrum.reshape(
        2, freq_groups, local_freqs, shot_count, receiver_groups, local_rows
    ).transpose(1, 4, 0, 2, 3, 5)
    spectrum = spectrum.reshape(
        freq_groups * receiver_groups, 2, local_freqs, shot_count, local_rows
    )
    received = lax.all_to_all(spectrum, ("freq", "rcv"), split_axis=0, concat_axis=0, tiled=True)
    right_side = received.transpose(1, 2, 0, 3, 4).reshape(2, local_freqs, -1, local_rows)
    counts = block_counts.reshape(-1)
    cols = block_cols.reshape(-1)
    ring = receiver_groups - 1
    up = [(i, i + 1) for i in range(ring)]
    down = [(i + 1, i) for i in range(ring)]

    def wide(value):
        return value[None, :, None, None]

    def own_part(t):
        lower = lax.ppermute(t[..., :rim], "rcv", down)
        upper = lax.ppermute(t[..., rim + local_rows : rim + local_rows + rim], "rcv", up)
        own = t[..., rim : rim + local_rows]
        own = own.at[..., :rim].add(upper)
        return own.at[..., local_rows - rim :].add(lower)

    def total(parts):
        return lax.psum(jnp.sum(parts, axis=tuple(range(1, parts.ndim))), "rcv")

    def square_sum(q):
        return lax.psum(jnp.sum(q * q, axis=(0, 2, 3)), "rcv")

    def extend(v):
        half = v.astype(jnp.bfloat16)
        below = lax.ppermute(half[..., local_rows - rim :], "rcv", up)
        above = lax.ppermute(half[..., :rim], "rcv", down)
        return jnp.concatenate(
            [below.astype(jnp.float32), v, above.astype(jnp.float32)], axis=-1
        )

    t, psq = operator_pass(counts, cols, down_blocks, start=right_side)
    beta = jnp.sqrt(total(psq) + EPSILON)
    q = own_part(t) / wide(beta)
    alpha = jnp.sqrt(square_sum(q) + EPSILON)
    v = q / wide(alpha)
    prev = right_side.astype(jnp.float32)
    w = v
    x = jnp.zeros_like(v)
    phibar = beta
    rhobar = alpha
    for iteration in range(ITERS):
        last = iteration == ITERS - 1
        prev, t, psq = operator_pass(
            counts, cols, down_blocks, field=extend(v), prev=prev, scale=alpha / beta
        )
        beta = jnp.sqrt(total(psq) + EPSILON)
        q = own_part(t) / wide(beta) - wide(beta) * v
        rho = jnp.sqrt(rhobar * rhobar + beta * beta)
        cosine = rhobar / rho
        sine = beta / rho
        phi = cosine * phibar
        phibar = sine * phibar
        x = x + wide(phi / rho) * w
        if last:
            return (x, wide(phibar * cosine) * q)
        alpha = jnp.sqrt(square_sum(q) + EPSILON)
        v = q / wide(alpha)
        theta = sine * alpha
        rhobar = -cosine * alpha
        w = v - wide(theta / rho) * w


def solution(mesh):
    return jax.shard_map(
        body,
        mesh=mesh,
        in_specs=(
            P(("freq", "rcv"), None, None),
            P("freq", "rcv", None, None, None, None),
            P("freq", "rcv", None),
            P("freq", "rcv"),
        ),
        out_specs=(P(None, "freq", None, "rcv"), P(None, "freq", None, "rcv")),
        check_vma=False,
    )
```

```python
import functools
import math

import jax
import jax.numpy as jnp
from jax import lax
from jax.experimental import pallas as pl
from jax.experimental.pallas import tpu as pltpu
from jax.sharding import PartitionSpec as P

ITERS = 2
EPSILON = 1e-06
GROUP = 4


def fourier_table(time_steps, freqs):
    shape = (time_steps, freqs)
    sample = lax.broadcasted_iota(jnp.int32, shape, 0)
    harmonic = lax.broadcasted_iota(jnp.int32, shape, 1) + 1
    phase_angle = 2.0 * math.pi / time_steps * (harmonic * sample % time_steps).astype(jnp.float32)
    scale_factor = 1.0 / math.sqrt(time_steps)
    return jnp.stack(
        [jnp.cos(phase_angle) * scale_factor, -jnp.sin(phase_angle) * scale_factor], axis=1
    ).astype(jnp.bfloat16)


def pass_kernel(first, dims, *refs):
    freqs, rows, slots, blk, reach, sources = dims
    if first:
        counts, cols, blocks, start, t, psq, buf, lhs, item_row, item_f, item_a, item_b, item_buf, sems = refs
    else:
        (counts, cols, blocks, field, stats, prev, p_out, t, psq,
         buf, lhs, item_row, item_f, item_a, item_b, item_buf, sems, zb, acc) = refs
    span = rows + 2 * reach
    pairs = (slots + 1) // 2
    total_rows = freqs * rows
    base = lax.axis_index("rcv") * rows - reach

    def lanes(index):
        return pl.ds(pl.multiple_of(index * blk, blk), blk)

    def copy_of(f, r, s0, item):
        return pltpu.make_async_copy(
            blocks.at[f, r, pl.ds(s0, 2)], buf.at[item], sems.at[item // GROUP]
        )

    total = jnp.int32(0)
    for f in range(freqs):
        def each_row(r, n, f=f):
            fr = f * rows + r
            count = counts[fr]
            here = (count + 1) // 2

            def each_pair(k, carry):
                item = n + k
                s0 = jnp.minimum(2 * k, slots - 2)
                copy_of(f, r, s0, item).start()
                item_row[item] = fr
                item_f[item] = f
                item_buf[item] = item
                item_a[item] = jnp.where(s0 == 2 * k, cols[fr * slots + s0] - base, span)
                item_b[item] = jnp.where(s0 + 1 < count, cols[fr * slots + s0 + 1] - base, span)
                return carry

            lax.fori_loop(0, here, each_pair, 0)
            return n + here

        total = lax.fori_loop(0, rows, each_row, total)
    for j in range(GROUP):
        item_row[total + j] = total_rows
        item_f[total + j] = 0
        item_buf[total + j] = 0
        item_a[total + j] = span
        item_b[total + j] = span
    groups = (total + GROUP - 1) // GROUP

    def arrive(g):
        for j in range(GROUP):
            @pl.when(g * GROUP + j < total)
            def _():
                copy_of(0, 0, 0, g * GROUP + j).wait()

    t[...] = jnp.zeros_like(t)
    lhs[total_rows] = jnp.zeros(lhs.shape[1:], lhs.dtype)
    if not first:
        inverse = 1.0 / stats[1]
        ratio = stats[1] / stats[0]
        for f in range(freqs):
            for c in range(2):
                scaled = field[c, f] * inverse[f : f + 1, :1]
                zb[c, f, :, : span * blk] = scaled.astype(jnp.bfloat16)
        zb[:, :, :, span * blk :] = jnp.zeros((2, freqs, sources, blk), jnp.bfloat16)
        acc[...] = jnp.zeros_like(acc)

        def forward(g, carry):
            arrive(g)
            for j in range(GROUP):
                i = g * GROUP + j
                f = item_f[i]
                za = zb[:, f, :, lanes(item_a[i])].reshape(2 * sources, blk)
                zc = zb[:, f, :, lanes(item_b[i])].reshape(2 * sources, blk)
                weights = buf[item_buf[i]].reshape(2, 2 * blk, blk)
                out = lax.dot_general(
                    jnp.concatenate([za, zc], axis=1),
                    jnp.concatenate([weights[0], weights[1]], axis=1),
                    (((1,), (1,)), ((), ())),
                    preferred_element_type=jnp.float32,
                )
                acc[item_row[i]] += out
            return carry

        lax.fori_loop(0, groups, forward, 0)

    for f in range(freqs):
        def finish(r, sums, f=f):
            fr = f * rows + r
            if first:
                real = start[0, f, :, lanes(r)]
                imag = start[1, f, :, lanes(r)]
                real16, imag16 = real, imag
                real, imag = real.astype(jnp.float32), imag.astype(jnp.float32)
            else:
                a = acc[fr]
                real = (
                    field[0, f, :, lanes(r + reach)] * inverse[f : f + 1, :]
                    + (a[:sources, :blk] - a[sources:, blk:])
                    - ratio[f : f + 1, :] * prev[0, f, :, lanes(r)]
                )
                imag = (
                    field[1, f, :, lanes(r + reach)] * inverse[f : f + 1, :]
                    + (a[:sources, blk:] + a[sources:, :blk])
                    - ratio[f : f + 1, :] * prev[1, f, :, lanes(r)]
                )
                p_out[0, f, :, lanes(r)] = real
                p_out[1, f, :, lanes(r)] = imag
                real16, imag16 = real.astype(jnp.bfloat16), imag.astype(jnp.bfloat16)
            t[0, f, :, lanes(r + reach)] = real
            t[1, f, :, lanes(r + reach)] = imag
            lhs[fr, :sources, :blk] = real16
            lhs[fr, :sources, blk:] = imag16
            lhs[fr, sources:, :blk] = imag16
            lhs[fr, sources:, blk:] = -real16
            squares = real * real + imag * imag
            return sums + jnp.sum(squares.reshape(sources // 8, 8, blk), axis=0)

        psq[f] = lax.fori_loop(0, rows, finish, jnp.zeros((8, blk), jnp.float32))

    def adjoint(g, carry):
        if first:
            arrive(g)
        for j in range(GROUP):
            i = g * GROUP + j
            f = item_f[i]
            weights = buf[item_buf[i]].reshape(2, 2 * blk, blk)
            out = jnp.dot(
                lhs[item_row[i]],
                jnp.concatenate([weights[0], weights[1]], axis=1),
                preferred_element_type=jnp.float32,
            )
            for index, half in ((item_a[i], out[:, :blk]), (item_b[i], out[:, blk:])):
                t[:, f, :, lanes(index)] += half.reshape(2, sources, blk)
        return carry

    lax.fori_loop(0, groups, adjoint, 0)


def operator_pass(counts, cols, blocks, start=None, field=None, stats=None, prev=None):
    freqs, rows, slots, _, blk, _ = blocks.shape
    first = start is not None
    sources = (start if first else prev).shape[2]
    reach = (slots - 1) // 2
    span = rows + 2 * reach
    pairs = (slots + 1) // 2
    items = freqs * rows * pairs
    dims = (freqs, rows, slots, blk, reach, sources)
    smem = pl.BlockSpec(memory_space=pltpu.SMEM)
    vmem = pl.BlockSpec(memory_space=pltpu.VMEM)
    hbm = pl.BlockSpec(memory_space=pl.ANY)
    t_shape = jax.ShapeDtypeStruct((2, freqs, sources, (span + 1) * blk), jnp.float32)
    psq_shape = jax.ShapeDtypeStruct((freqs, 8, blk), jnp.float32)
    listed = (items + GROUP,)
    scratch = [
        pltpu.VMEM((items, 2, 2, blk, blk), jnp.bfloat16),
        pltpu.VMEM((freqs * rows + 1, 2 * sources, 2 * blk), jnp.bfloat16),
        pltpu.SMEM(listed, jnp.int32),
        pltpu.SMEM(listed, jnp.int32),
        pltpu.SMEM(listed, jnp.int32),
        pltpu.SMEM(listed, jnp.int32),
        pltpu.SMEM(listed, jnp.int32),
        pltpu.SemaphoreType.DMA(((items + GROUP - 1) // GROUP,)),
    ]
    if first:
        args = (counts, cols, blocks, start)
        in_specs = [smem, smem, hbm, vmem]
        out_shape = (t_shape, psq_shape)
    else:
        args = (counts, cols, blocks, field, stats, prev)
        in_specs = [smem, smem, hbm, vmem, vmem, vmem]
        out_shape = (jax.ShapeDtypeStruct(prev.shape, jnp.float32), t_shape, psq_shape)
        scratch += [
            pltpu.VMEM((2, freqs, sources, (span + 1) * blk), jnp.bfloat16),
            pltpu.VMEM((freqs * rows + 1, 2 * sources, 2 * blk), jnp.float32),
        ]
    return pl.pallas_call(
        functools.partial(pass_kernel, first, dims),
        out_shape=out_shape,
        in_specs=in_specs,
        out_specs=tuple(vmem for _ in out_shape),
        scratch_shapes=scratch,
        compiler_params=pltpu.CompilerParams(vmem_limit_bytes=56 * 1024 * 1024),
        name="first_adjoint" if first else "forward_adjoint",
    )(*args)


def exchange_kernel(first, last, dims, *refs):
    freqs, rows, blk, reach, peers = dims
    t, psq, refs = refs[0], refs[1], refs[2:]
    if not first:
        before, stats_before, refs = refs[0], refs[1], refs[2:]
    q, stats, refs = refs[0], refs[1], refs[2:]
    (send_lo, send_hi, from_lo, from_hi, mine, theirs,
     rim_send, rim_recv, sum_send, sum_recv) = refs
    me = lax.axis_index("rcv")
    two = 2 * reach * blk
    rim = reach * blk
    span = (rows + 2 * reach) * blk
    has_lo = me > 0
    has_hi = me < peers - 1

    barrier = pltpu.get_barrier_semaphore()
    for d in range(1, peers):
        pl.semaphore_signal(
            barrier, inc=1, device_id={"rcv": lax.rem(me + d, peers)},
            device_id_type=pl.DeviceIdType.MESH,
        )
    send_lo[...] = t[:, :, :, :two].astype(jnp.bfloat16)
    send_hi[...] = t[:, :, :, span - two : span].astype(jnp.bfloat16)

    def to_row(parts):
        rows_of = [jnp.sum(part, axis=0, keepdims=True) for part in parts]
        rows_of.append(jnp.zeros((8 - len(parts), blk), jnp.float32))
        return jnp.concatenate(rows_of, axis=0)

    mine[0] = to_row([psq[f] for f in range(freqs)])
    pl.semaphore_wait(barrier, peers - 1)

    def sum_copy(k, d):
        return pltpu.make_async_remote_copy(
            src_ref=mine.at[k], dst_ref=theirs.at[k, d - 1],
            send_sem=sum_send.at[k, d - 1], recv_sem=sum_recv.at[k, d - 1],
            device_id={"rcv": lax.rem(me + d, peers)}, device_id_type=pl.DeviceIdType.MESH,
        )

    def lo_copy():
        return pltpu.make_async_remote_copy(
            src_ref=send_lo, dst_ref=from_hi, send_sem=rim_send.at[0], recv_sem=rim_recv.at[1],
            device_id={"rcv": lax.rem(me + peers - 1, peers)}, device_id_type=pl.DeviceIdType.MESH,
        )

    def hi_copy():
        return pltpu.make_async_remote_copy(
            src_ref=send_hi, dst_ref=from_lo, send_sem=rim_send.at[1], recv_sem=rim_recv.at[0],
            device_id={"rcv": lax.rem(me + 1, peers)}, device_id_type=pl.DeviceIdType.MESH,
        )

    for d in range(1, peers):
        sum_copy(0, d).start()

    @pl.when(has_lo)
    def _():
        lo_copy().start()

    @pl.when(has_hi)
    def _():
        hi_copy().start()

    @pl.when(jnp.logical_not(has_lo))
    def _():
        from_lo[...] = jnp.zeros_like(from_lo)

    @pl.when(jnp.logical_not(has_hi))
    def _():
        from_hi[...] = jnp.zeros_like(from_hi)

    def norm(k):
        total = mine[k]
        for d in range(1, peers):
            sum_copy(k, d).wait_recv()
        for d in range(1, peers):
            total += theirs[k, d - 1]
        value = jnp.sqrt(jnp.sum(total, axis=1, keepdims=True) + EPSILON)
        return jnp.broadcast_to(value, (8, blk))

    beta = norm(0)
    stats[0] = beta
    by_beta = 1.0 / beta
    if not first:
        pull = beta / stats_before[1]
    sums = [jnp.zeros((8, blk), jnp.float32) for _ in range(freqs)]

    def sweep(low, high, extra, offset):
        own = low >= rim and high <= span - rim
        if last and not own:
            return
        shift = rim if last else 0
        for f in range(freqs):
            for c in range(2):
                value = t[c, f, :, low:high]
                if extra is not None:
                    value += extra[c, f, :, offset : offset + high - low].astype(jnp.float32)
                value = value * by_beta[f : f + 1, :1]
                if not first:
                    value -= before[c, f, :, low:high] * pull[f : f + 1, :1]
                q[c, f, :, low - shift : high - shift] = value
                if own and not last:
                    squares = value * value
                    for j in range(0, high - low, blk):
                        part = squares[:, j : j + blk]
                        sums[f] = sums[f] + jnp.sum(part.reshape(-1, 8, blk), axis=0)

    if span > 2 * two:
        for low in range(two, span - two, rim):
            sweep(low, min(low + rim, span - two), None, 0)

    @pl.when(has_lo)
    def _():
        hi_like = pltpu.make_async_remote_copy(
            src_ref=send_hi, dst_ref=from_lo, send_sem=rim_send.at[1], recv_sem=rim_recv.at[0],
            device_id={"rcv": lax.rem(me + 1, peers)}, device_id_type=pl.DeviceIdType.MESH,
        )
        hi_like.wait_recv()

    sweep(rim, two, from_lo, rim)

    @pl.when(has_hi)
    def _():
        lo_copy().wait_recv()

    sweep(span - two, span - rim, from_hi, 0)
    if not last:
        mine[1] = to_row(sums)
        for d in range(1, peers):
            sum_copy(1, d).start()
        sweep(0, rim, from_lo, 0)
        sweep(span - rim, span, from_hi, rim)
        stats[1] = norm(1)
    for d in range(1, peers):
        sum_copy(0, d).wait_send()
        if not last:
            sum_copy(1, d).wait_send()

    @pl.when(has_lo)
    def _():
        lo_copy().wait_send()

    @pl.when(has_hi)
    def _():
        hi_copy().wait_send()


def exchange(t, psq, before, stats_before, dims, last):
    freqs, rows, blk, reach, peers = dims
    first = before is None
    sources = t.shape[2]
    vmem = pl.BlockSpec(memory_space=pltpu.VMEM)
    lanes = rows * blk if last else (rows + 2 * reach) * blk
    args = (t, psq) if first else (t, psq, before, stats_before)
    rim = pltpu.VMEM((2, freqs, sources, 2 * reach * blk), jnp.bfloat16)
    return pl.pallas_call(
        functools.partial(exchange_kernel, first, last, dims),
        out_shape=(
            jax.ShapeDtypeStruct((2, freqs, sources, lanes), jnp.float32),
            jax.ShapeDtypeStruct((2, 8, blk), jnp.float32),
        ),
        in_specs=[vmem] * len(args),
        out_specs=(vmem, vmem),
        scratch_shapes=[
            rim, rim, rim, rim,
            pltpu.VMEM((2, 8, blk), jnp.float32),
            pltpu.VMEM((2, peers - 1, 8, blk), jnp.float32),
            pltpu.SemaphoreType.DMA((2,)),
            pltpu.SemaphoreType.DMA((2,)),
            pltpu.SemaphoreType.DMA((2, peers - 1)),
            pltpu.SemaphoreType.DMA((2, peers - 1)),
        ],
        compiler_params=pltpu.CompilerParams(
            collective_id=0 if first else (2 if last else 1),
            has_side_effects=True,
            vmem_limit_bytes=32 * 1024 * 1024,
        ),
        name="exchange",
    )(*args)


def body(up_time, down_blocks, block_cols, block_counts):
    freq_groups = lax.axis_size("freq")
    receiver_groups = lax.axis_size("rcv")
    shot_count, time_steps, receivers = up_time.shape
    local_freqs, local_blocks, slot_count, _, block_size, _ = down_blocks.shape
    local_rows = receivers // receiver_groups
    reach_blocks = (slot_count - 1) // 2
    rim = reach_blocks * block_size
    fourier = fourier_table(time_steps, freq_groups * local_freqs)
    fourier = fourier.reshape(time_steps, -1).T
    spectrum = jnp.stack(
        [
            jnp.dot(fourier, up_time[s], preferred_element_type=jnp.float32).astype(jnp.bfloat16)
            for s in range(shot_count)
        ],
        axis=1,
    )
    spectrum = spectrum.reshape(
        2, freq_groups, local_freqs, shot_count, receiver_groups, local_rows
    ).transpose(1, 4, 0, 2, 3, 5)
    spectrum = spectrum.reshape(
        freq_groups * receiver_groups, 2, local_freqs, shot_count, local_rows
    )
    received = lax.all_to_all(spectrum, ("freq", "rcv"), split_axis=0, concat_axis=0, tiled=True)
    right_side = received.transpose(1, 2, 0, 3, 4).reshape(2, local_freqs, -1, local_rows)
    counts = block_counts.reshape(-1)
    cols = block_cols.reshape(-1)
    ring = receiver_groups - 1
    up = [(i, i + 1) for i in range(ring)]
    down = [(i + 1, i) for i in range(ring)]

    def wide(value):
        return value[None, :, None, None]

    def stats_of(beta, alpha):
        rows = jnp.pad(jnp.stack([beta, alpha]), ((0, 0), (0, 8 - local_freqs)), constant_values=1.0)
        return jnp.broadcast_to(rows[:, :, None], (2, 8, block_size))

    def plain_exchange(t, psq, before, stats_before, last):
        lower = lax.ppermute(t[..., :rim], "rcv", down)
        upper = lax.ppermute(t[..., rim + local_rows : rim + local_rows + rim], "rcv", up)
        q = t[..., rim : rim + local_rows]
        q = q.at[..., :rim].add(upper)
        q = q.at[..., local_rows - rim :].add(lower)
        beta = jnp.sqrt(lax.psum(jnp.sum(psq, axis=(1, 2)), "rcv") + EPSILON)
        q = q / wide(beta)
        if before is not None:
            own = before[..., rim : rim + local_rows]
            q = q - wide(beta / stats_before[1, :local_freqs, 0]) * own
        if last:
            return q, stats_of(beta, beta)
        alpha = jnp.sqrt(lax.psum(jnp.sum(q * q, axis=(0, 2, 3)), "rcv") + EPSILON)
        below = lax.ppermute(q[..., local_rows - rim :], "rcv", up)
        above = lax.ppermute(q[..., :rim], "rcv", down)
        return jnp.concatenate([below, q, above], axis=-1), stats_of(beta, alpha)

    def step(t, psq, before, stats_before, last):
        if local_blocks < 2 * reach_blocks:
            return plain_exchange(t, psq, before, stats_before, last)
        dims = (local_freqs, local_blocks, block_size, reach_blocks, receiver_groups)
        return exchange(t, psq, before, stats_before, dims, last)

    t, psq = operator_pass(counts, cols, down_blocks, start=right_side)
    prev = right_side.astype(jnp.float32)
    q, stats = step(t, psq, None, None, False)
    fields, norms = [q], [stats]
    for iteration in range(ITERS):
        prev, t, psq = operator_pass(
            counts, cols, down_blocks, field=q, stats=stats, prev=prev
        )
        q, stats = step(t, psq, q, stats, iteration == ITERS - 1)
        fields.append(q)
        norms.append(stats)

    betas = [stats[0, :local_freqs, 0] for stats in norms]
    alphas = [stats[1, :local_freqs, 0] for stats in norms]
    phibar = betas[0]
    rhobar = alphas[0]
    weights = [jnp.zeros_like(phibar) for _ in range(ITERS)]
    direction = [1.0 / alphas[0]]
    for iteration in range(ITERS):
        beta = betas[iteration + 1]
        rho = jnp.sqrt(rhobar * rhobar + beta * beta)
        cosine = rhobar / rho
        sine = beta / rho
        phi = cosine * phibar
        phibar = sine * phibar
        for i, part in enumerate(direction):
            weights[i] = weights[i] + phi / rho * part
        if iteration == ITERS - 1:
            break
        alpha = alphas[iteration + 1]
        theta = sine * alpha
        rhobar = -cosine * alpha
        direction = [-theta / rho * part for part in direction] + [1.0 / alpha]
    x = sum(
        wide(weight) * field[..., rim : rim + local_rows]
        for weight, field in zip(weights, fields)
    )
    return (x, wide(phibar * cosine) * q)


def solution(mesh):
    return jax.shard_map(
        body,
        mesh=mesh,
        in_specs=(
            P(("freq", "rcv"), None, None),
            P("freq", "rcv", None, None, None, None),
            P("freq", "rcv", None),
            P("freq", "rcv"),
        ),
        out_specs=(P(None, "freq", None, "rcv"), P(None, "freq", None, "rcv")),
        check_vma=False,
    )
```

```python
import functools
import math

import jax
import jax.numpy as jnp
from jax import lax
from jax.experimental import pallas as pl
from jax.experimental.pallas import tpu as pltpu
from jax.sharding import PartitionSpec as P

ITERS = 2
EPSILON = 1e-06
GROUP = 16


def fourier_table(time_steps, freqs):
    shape = (time_steps, freqs)
    sample = lax.broadcasted_iota(jnp.int32, shape, 0)
    harmonic = lax.broadcasted_iota(jnp.int32, shape, 1) + 1
    phase_angle = 2.0 * math.pi / time_steps * (harmonic * sample % time_steps).astype(jnp.float32)
    scale_factor = 1.0 / math.sqrt(time_steps)
    return jnp.stack(
        [jnp.cos(phase_angle) * scale_factor, -jnp.sin(phase_angle) * scale_factor], axis=1
    ).astype(jnp.bfloat16)


def pass_kernel(first, dims, *refs):
    freqs, rows, slots, blk, reach, sources = dims
    if first:
        counts, cols, blocks, start, t, psq, buf, lhs, item_row, item_f, item_a, item_b, item_buf, sems = refs
    else:
        (counts, cols, blocks, field, stats, prev, p_out, t, psq,
         buf, lhs, item_row, item_f, item_a, item_b, item_buf, sems, zb, acc) = refs
    span = rows + 2 * reach
    pairs = (slots + 1) // 2
    total_rows = freqs * rows
    base = lax.axis_index("rcv") * rows - reach

    def lanes(index):
        return pl.ds(pl.multiple_of(index * blk, blk), blk)

    def copy_of(f, r, s0, item):
        return pltpu.make_async_copy(
            blocks.at[f, r, pl.ds(s0, 2)], buf.at[item], sems.at[item // GROUP]
        )

    total = jnp.int32(0)
    for f in range(freqs):
        def each_row(r, n, f=f):
            fr = f * rows + r
            count = counts[fr]
            here = (count + 1) // 2

            def each_pair(k, carry):
                item = n + k
                s0 = jnp.minimum(2 * k, slots - 2)
                copy_of(f, r, s0, item).start()
                item_row[item] = fr
                item_f[item] = f
                item_buf[item] = item
                item_a[item] = jnp.where(s0 == 2 * k, cols[fr * slots + s0] - base, span)
                item_b[item] = jnp.where(s0 + 1 < count, cols[fr * slots + s0 + 1] - base, span)
                return carry

            lax.fori_loop(0, here, each_pair, 0)
            return n + here

        total = lax.fori_loop(0, rows, each_row, total)
    for j in range(GROUP):
        item_row[total + j] = total_rows
        item_f[total + j] = 0
        item_buf[total + j] = 0
        item_a[total + j] = span
        item_b[total + j] = span
    groups = (total + GROUP - 1) // GROUP

    def arrive(g):
        for j in range(GROUP):
            @pl.when(g * GROUP + j < total)
            def _():
                copy_of(0, 0, 0, g * GROUP + j).wait()

    t[...] = jnp.zeros_like(t)
    lhs[total_rows] = jnp.zeros(lhs.shape[1:], lhs.dtype)
    if not first:
        inverse = 1.0 / stats[1]
        ratio = stats[1] / stats[0]
        for f in range(freqs):
            for c in range(2):
                scaled = field[c, f] * inverse[f : f + 1, :1]
                zb[c, f, :, : span * blk] = scaled.astype(jnp.bfloat16)
        zb[:, :, :, span * blk :] = jnp.zeros((2, freqs, sources, blk), jnp.bfloat16)
        acc[...] = jnp.zeros_like(acc)

        def forward(g, carry):
            arrive(g)
            for j in range(GROUP):
                i = g * GROUP + j
                f = item_f[i]
                za = zb[:, f, :, lanes(item_a[i])].reshape(2 * sources, blk)
                zc = zb[:, f, :, lanes(item_b[i])].reshape(2 * sources, blk)
                weights = buf[item_buf[i]].reshape(2, 2 * blk, blk)
                out = lax.dot_general(
                    jnp.concatenate([za, zc], axis=1),
                    jnp.concatenate([weights[0], weights[1]], axis=1),
                    (((1,), (1,)), ((), ())),
                    preferred_element_type=jnp.float32,
                )
                acc[item_row[i]] += out
            return carry

        lax.fori_loop(0, groups, forward, 0)

    for f in range(freqs):
        def finish(r, sums, f=f):
            fr = f * rows + r
            if first:
                real = start[0, f, :, lanes(r)]
                imag = start[1, f, :, lanes(r)]
                real16, imag16 = real, imag
                real, imag = real.astype(jnp.float32), imag.astype(jnp.float32)
            else:
                a = acc[fr]
                real = (
                    field[0, f, :, lanes(r + reach)] * inverse[f : f + 1, :]
                    + (a[:sources, :blk] - a[sources:, blk:])
                    - ratio[f : f + 1, :] * prev[0, f, :, lanes(r)]
                )
                imag = (
                    field[1, f, :, lanes(r + reach)] * inverse[f : f + 1, :]
                    + (a[:sources, blk:] + a[sources:, :blk])
                    - ratio[f : f + 1, :] * prev[1, f, :, lanes(r)]
                )
                p_out[0, f, :, lanes(r)] = real
                p_out[1, f, :, lanes(r)] = imag
                real16, imag16 = real.astype(jnp.bfloat16), imag.astype(jnp.bfloat16)
            t[0, f, :, lanes(r + reach)] = real
            t[1, f, :, lanes(r + reach)] = imag
            lhs[fr, :sources, :blk] = real16
            lhs[fr, :sources, blk:] = imag16
            lhs[fr, sources:, :blk] = imag16
            lhs[fr, sources:, blk:] = -real16
            squares = real * real + imag * imag
            return sums + jnp.sum(squares.reshape(sources // 8, 8, blk), axis=0)

        psq[f] = lax.fori_loop(0, rows, finish, jnp.zeros((8, blk), jnp.float32))

    def adjoint(g, carry):
        if first:
            arrive(g)
        for j in range(GROUP):
            i = g * GROUP + j
            f = item_f[i]
            weights = buf[item_buf[i]].reshape(2, 2 * blk, blk)
            out = jnp.dot(
                lhs[item_row[i]],
                jnp.concatenate([weights[0], weights[1]], axis=1),
                preferred_element_type=jnp.float32,
            )
            for index, half in ((item_a[i], out[:, :blk]), (item_b[i], out[:, blk:])):
                t[:, f, :, lanes(index)] += half.reshape(2, sources, blk)
        return carry

    lax.fori_loop(0, groups, adjoint, 0)


def operator_pass(counts, cols, blocks, start=None, field=None, stats=None, prev=None):
    freqs, rows, slots, _, blk, _ = blocks.shape
    first = start is not None
    sources = (start if first else prev).shape[2]
    reach = (slots - 1) // 2
    span = rows + 2 * reach
    pairs = (slots + 1) // 2
    items = freqs * rows * pairs
    dims = (freqs, rows, slots, blk, reach, sources)
    smem = pl.BlockSpec(memory_space=pltpu.SMEM)
    vmem = pl.BlockSpec(memory_space=pltpu.VMEM)
    hbm = pl.BlockSpec(memory_space=pl.ANY)
    t_shape = jax.ShapeDtypeStruct((2, freqs, sources, (span + 1) * blk), jnp.float32)
    psq_shape = jax.ShapeDtypeStruct((freqs, 8, blk), jnp.float32)
    listed = (items + GROUP,)
    scratch = [
        pltpu.VMEM((items, 2, 2, blk, blk), jnp.bfloat16),
        pltpu.VMEM((freqs * rows + 1, 2 * sources, 2 * blk), jnp.bfloat16),
        pltpu.SMEM(listed, jnp.int32),
        pltpu.SMEM(listed, jnp.int32),
        pltpu.SMEM(listed, jnp.int32),
        pltpu.SMEM(listed, jnp.int32),
        pltpu.SMEM(listed, jnp.int32),
        pltpu.SemaphoreType.DMA(((items + GROUP - 1) // GROUP,)),
    ]
    if first:
        args = (counts, cols, blocks, start)
        in_specs = [smem, smem, hbm, vmem]
        out_shape = (t_shape, psq_shape)
    else:
        args = (counts, cols, blocks, field, stats, prev)
        in_specs = [smem, smem, hbm, vmem, vmem, vmem]
        out_shape = (jax.ShapeDtypeStruct(prev.shape, jnp.float32), t_shape, psq_shape)
        scratch += [
            pltpu.VMEM((2, freqs, sources, (span + 1) * blk), jnp.bfloat16),
            pltpu.VMEM((freqs * rows + 1, 2 * sources, 2 * blk), jnp.float32),
        ]
    return pl.pallas_call(
        functools.partial(pass_kernel, first, dims),
        out_shape=out_shape,
        in_specs=in_specs,
        out_specs=tuple(vmem for _ in out_shape),
        scratch_shapes=scratch,
        compiler_params=pltpu.CompilerParams(vmem_limit_bytes=46 * 1024 * 1024),
        name="first_adjoint" if first else "forward_adjoint",
    )(*args)


def exchange_kernel(first, last, dims, *refs):
    freqs, rows, blk, reach, peers = dims
    t, psq, refs = refs[0], refs[1], refs[2:]
    if not first:
        before, stats_before, refs = refs[0], refs[1], refs[2:]
    q, stats, refs = refs[0], refs[1], refs[2:]
    (send_lo, send_hi, from_lo, from_hi, mine, theirs,
     rim_send, rim_recv, sum_send, sum_recv) = refs
    me = lax.axis_index("rcv")
    two = 2 * reach * blk
    rim = reach * blk
    span = (rows + 2 * reach) * blk
    has_lo = me > 0
    has_hi = me < peers - 1

    barrier = pltpu.get_barrier_semaphore()
    for d in range(1, peers):
        pl.semaphore_signal(
            barrier, inc=1, device_id={"rcv": lax.rem(me + d, peers)},
            device_id_type=pl.DeviceIdType.MESH,
        )
    send_lo[...] = t[:, :, :, :two].astype(jnp.bfloat16)
    send_hi[...] = t[:, :, :, span - two : span].astype(jnp.bfloat16)

    def to_row(parts):
        rows_of = [jnp.sum(part, axis=0, keepdims=True) for part in parts]
        rows_of.append(jnp.zeros((8 - len(parts), blk), jnp.float32))
        return jnp.concatenate(rows_of, axis=0)

    mine[0] = to_row([psq[f] for f in range(freqs)])
    pl.semaphore_wait(barrier, peers - 1)

    def sum_copy(k, d):
        return pltpu.make_async_remote_copy(
            src_ref=mine.at[k], dst_ref=theirs.at[k, d - 1],
            send_sem=sum_send.at[k, d - 1], recv_sem=sum_recv.at[k, d - 1],
            device_id={"rcv": lax.rem(me + d, peers)}, device_id_type=pl.DeviceIdType.MESH,
        )

    def lo_copy():
        return pltpu.make_async_remote_copy(
            src_ref=send_lo, dst_ref=from_hi, send_sem=rim_send.at[0], recv_sem=rim_recv.at[1],
            device_id={"rcv": lax.rem(me + peers - 1, peers)}, device_id_type=pl.DeviceIdType.MESH,
        )

    def hi_copy():
        return pltpu.make_async_remote_copy(
            src_ref=send_hi, dst_ref=from_lo, send_sem=rim_send.at[1], recv_sem=rim_recv.at[0],
            device_id={"rcv": lax.rem(me + 1, peers)}, device_id_type=pl.DeviceIdType.MESH,
        )

    for d in range(1, peers):
        sum_copy(0, d).start()

    @pl.when(has_lo)
    def _():
        lo_copy().start()

    @pl.when(has_hi)
    def _():
        hi_copy().start()

    @pl.when(jnp.logical_not(has_lo))
    def _():
        from_lo[...] = jnp.zeros_like(from_lo)

    @pl.when(jnp.logical_not(has_hi))
    def _():
        from_hi[...] = jnp.zeros_like(from_hi)

    def norm(k):
        total = mine[k]
        for d in range(1, peers):
            sum_copy(k, d).wait_recv()
        for d in range(1, peers):
            total += theirs[k, d - 1]
        value = jnp.sqrt(jnp.sum(total, axis=1, keepdims=True) + EPSILON)
        return jnp.broadcast_to(value, (8, blk))

    beta = norm(0)
    stats[0] = beta
    by_beta = 1.0 / beta
    if not first:
        pull = beta / stats_before[1]
    sums = [jnp.zeros((8, blk), jnp.float32) for _ in range(freqs)]

    def sweep(low, high, extra, offset):
        own = low >= rim and high <= span - rim
        if last and not own:
            return
        shift = rim if last else 0
        for f in range(freqs):
            for c in range(2):
                value = t[c, f, :, low:high]
                if extra is not None:
                    value += extra[c, f, :, offset : offset + high - low].astype(jnp.float32)
                value = value * by_beta[f : f + 1, :1]
                if not first:
                    value -= before[c, f, :, low:high] * pull[f : f + 1, :1]
                q[c, f, :, low - shift : high - shift] = value
                if own and not last:
                    squares = value * value
                    for j in range(0, high - low, blk):
                        part = squares[:, j : j + blk]
                        sums[f] = sums[f] + jnp.sum(part.reshape(-1, 8, blk), axis=0)

    if span > 2 * two:
        for low in range(two, span - two, rim):
            sweep(low, min(low + rim, span - two), None, 0)

    @pl.when(has_lo)
    def _():
        hi_like = pltpu.make_async_remote_copy(
            src_ref=send_hi, dst_ref=from_lo, send_sem=rim_send.at[1], recv_sem=rim_recv.at[0],
            device_id={"rcv": lax.rem(me + 1, peers)}, device_id_type=pl.DeviceIdType.MESH,
        )
        hi_like.wait_recv()

    sweep(rim, two, from_lo, rim)

    @pl.when(has_hi)
    def _():
        lo_copy().wait_recv()

    sweep(span - two, span - rim, from_hi, 0)
    if not last:
        mine[1] = to_row(sums)
        for d in range(1, peers):
            sum_copy(1, d).start()
        sweep(0, rim, from_lo, 0)
        sweep(span - rim, span, from_hi, rim)
        stats[1] = norm(1)
    for d in range(1, peers):
        sum_copy(0, d).wait_send()
        if not last:
            sum_copy(1, d).wait_send()

    @pl.when(has_lo)
    def _():
        lo_copy().wait_send()

    @pl.when(has_hi)
    def _():
        hi_copy().wait_send()


def exchange(t, psq, before, stats_before, dims, last):
    freqs, rows, blk, reach, peers = dims
    first = before is None
    sources = t.shape[2]
    vmem = pl.BlockSpec(memory_space=pltpu.VMEM)
    lanes = rows * blk if last else (rows + 2 * reach) * blk
    args = (t, psq) if first else (t, psq, before, stats_before)
    rim = pltpu.VMEM((2, freqs, sources, 2 * reach * blk), jnp.bfloat16)
    return pl.pallas_call(
        functools.partial(exchange_kernel, first, last, dims),
        out_shape=(
            jax.ShapeDtypeStruct((2, freqs, sources, lanes), jnp.float32),
            jax.ShapeDtypeStruct((2, 8, blk), jnp.float32),
        ),
        in_specs=[vmem] * len(args),
        out_specs=(vmem, vmem),
        scratch_shapes=[
            rim, rim, rim, rim,
            pltpu.VMEM((2, 8, blk), jnp.float32),
            pltpu.VMEM((2, peers - 1, 8, blk), jnp.float32),
            pltpu.SemaphoreType.DMA((2,)),
            pltpu.SemaphoreType.DMA((2,)),
            pltpu.SemaphoreType.DMA((2, peers - 1)),
            pltpu.SemaphoreType.DMA((2, peers - 1)),
        ],
        compiler_params=pltpu.CompilerParams(
            collective_id=0 if first else (2 if last else 1),
            has_side_effects=True,
            vmem_limit_bytes=16 * 1024 * 1024,
        ),
        name="exchange",
    )(*args)


def body(up_time, down_blocks, block_cols, block_counts):
    freq_groups = lax.axis_size("freq")
    receiver_groups = lax.axis_size("rcv")
    shot_count, time_steps, receivers = up_time.shape
    local_freqs, local_blocks, slot_count, _, block_size, _ = down_blocks.shape
    local_rows = receivers // receiver_groups
    reach_blocks = (slot_count - 1) // 2
    rim = reach_blocks * block_size
    fourier = fourier_table(time_steps, freq_groups * local_freqs)
    fourier = fourier.reshape(time_steps, -1).T
    spectrum = jnp.stack(
        [
            jnp.dot(fourier, up_time[s], preferred_element_type=jnp.float32).astype(jnp.bfloat16)
            for s in range(shot_count)
        ],
        axis=1,
    )
    spectrum = spectrum.reshape(
        2, freq_groups, local_freqs, shot_count, receiver_groups, local_rows
    ).transpose(1, 4, 0, 2, 3, 5)
    spectrum = spectrum.reshape(
        freq_groups * receiver_groups, 2, local_freqs, shot_count, local_rows
    )
    received = lax.all_to_all(spectrum, ("freq", "rcv"), split_axis=0, concat_axis=0, tiled=True)
    right_side = received.transpose(1, 2, 0, 3, 4).reshape(2, local_freqs, -1, local_rows)
    counts = block_counts.reshape(-1)
    cols = block_cols.reshape(-1)
    ring = receiver_groups - 1
    up = [(i, i + 1) for i in range(ring)]
    down = [(i + 1, i) for i in range(ring)]

    def wide(value):
        return value[None, :, None, None]

    def stats_of(beta, alpha):
        rows = jnp.pad(jnp.stack([beta, alpha]), ((0, 0), (0, 8 - local_freqs)), constant_values=1.0)
        return jnp.broadcast_to(rows[:, :, None], (2, 8, block_size))

    def plain_exchange(t, psq, before, stats_before, last):
        lower = lax.ppermute(t[..., :rim], "rcv", down)
        upper = lax.ppermute(t[..., rim + local_rows : rim + local_rows + rim], "rcv", up)
        q = t[..., rim : rim + local_rows]
        q = q.at[..., :rim].add(upper)
        q = q.at[..., local_rows - rim :].add(lower)
        beta = jnp.sqrt(lax.psum(jnp.sum(psq, axis=(1, 2)), "rcv") + EPSILON)
        q = q / wide(beta)
        if before is not None:
            own = before[..., rim : rim + local_rows]
            q = q - wide(beta / stats_before[1, :local_freqs, 0]) * own
        if last:
            return q, stats_of(beta, beta)
        alpha = jnp.sqrt(lax.psum(jnp.sum(q * q, axis=(0, 2, 3)), "rcv") + EPSILON)
        below = lax.ppermute(q[..., local_rows - rim :], "rcv", up)
        above = lax.ppermute(q[..., :rim], "rcv", down)
        return jnp.concatenate([below, q, above], axis=-1), stats_of(beta, alpha)

    def step(t, psq, before, stats_before, last):
        if local_blocks < 2 * reach_blocks:
            return plain_exchange(t, psq, before, stats_before, last)
        dims = (local_freqs, local_blocks, block_size, reach_blocks, receiver_groups)
        return exchange(t, psq, before, stats_before, dims, last)

    t, psq = operator_pass(counts, cols, down_blocks, start=right_side)
    prev = right_side.astype(jnp.float32)
    q, stats = step(t, psq, None, None, False)
    fields, norms = [q], [stats]
    for iteration in range(ITERS):
        prev, t, psq = operator_pass(
            counts, cols, down_blocks, field=q, stats=stats, prev=prev
        )
        q, stats = step(t, psq, q, stats, iteration == ITERS - 1)
        fields.append(q)
        norms.append(stats)

    betas = [stats[0, :local_freqs, 0] for stats in norms]
    alphas = [stats[1, :local_freqs, 0] for stats in norms]
    phibar = betas[0]
    rhobar = alphas[0]
    weights = [jnp.zeros_like(phibar) for _ in range(ITERS)]
    direction = [1.0 / alphas[0]]
    for iteration in range(ITERS):
        beta = betas[iteration + 1]
        rho = jnp.sqrt(rhobar * rhobar + beta * beta)
        cosine = rhobar / rho
        sine = beta / rho
        phi = cosine * phibar
        phibar = sine * phibar
        for i, part in enumerate(direction):
            weights[i] = weights[i] + phi / rho * part
        if iteration == ITERS - 1:
            break
        alpha = alphas[iteration + 1]
        theta = sine * alpha
        rhobar = -cosine * alpha
        direction = [-theta / rho * part for part in direction] + [1.0 / alpha]
    x = sum(
        wide(weight) * field[..., rim : rim + local_rows]
        for weight, field in zip(weights, fields)
    )
    return (x, wide(phibar * cosine) * q)


def solution(mesh):
    return jax.shard_map(
        body,
        mesh=mesh,
        in_specs=(
            P(("freq", "rcv"), None, None),
            P("freq", "rcv", None, None, None, None),
            P("freq", "rcv", None),
            P("freq", "rcv"),
        ),
        out_specs=(P(None, "freq", None, "rcv"), P(None, "freq", None, "rcv")),
        check_vma=False,
    )
```

```python
import functools
import math

import jax
import jax.numpy as jnp
from jax import lax
from jax.experimental import pallas as pl
from jax.experimental.pallas import tpu as pltpu
from jax.sharding import PartitionSpec as P

ITERS = 2
EPSILON = 1e-06
GROUP = 16


def fourier_table(time_steps, freqs):
    shape = (time_steps, freqs)
    sample = lax.broadcasted_iota(jnp.int32, shape, 0)
    harmonic = lax.broadcasted_iota(jnp.int32, shape, 1) + 1
    phase_angle = 2.0 * math.pi / time_steps * (harmonic * sample % time_steps).astype(jnp.float32)
    scale_factor = 1.0 / math.sqrt(time_steps)
    return jnp.stack(
        [jnp.cos(phase_angle) * scale_factor, -jnp.sin(phase_angle) * scale_factor], axis=1
    ).astype(jnp.bfloat16)


def pass_kernel(first, dims, *refs):
    freqs, rows, slots, blk, reach, sources = dims
    if first:
        counts, cols, blocks, start, t, psq, buf, lhs, item_row, item_f, item_a, item_b, item_buf, sems = refs
    else:
        (counts, cols, blocks, field, stats, prev, p_out, t, psq,
         buf, lhs, item_row, item_f, item_a, item_b, item_buf, sems, zb, acc) = refs
    span = rows + 2 * reach
    pairs = (slots + 1) // 2
    total_rows = freqs * rows
    base = lax.axis_index("rcv") * rows - reach

    def lanes(index):
        return pl.ds(pl.multiple_of(index * blk, blk), blk)

    def copy_of(f, r, s0, item):
        return pltpu.make_async_copy(
            blocks.at[f, r, pl.ds(s0, 2)], buf.at[item], sems.at[item // GROUP]
        )

    total = jnp.int32(0)
    for f in range(freqs):
        def each_row(r, n, f=f):
            fr = f * rows + r
            count = counts[fr]
            here = (count + 1) // 2

            def each_pair(k, carry):
                item = n + k
                s0 = jnp.minimum(2 * k, slots - 2)
                copy_of(f, r, s0, item).start()
                item_row[item] = fr
                item_f[item] = f
                item_buf[item] = item
                item_a[item] = jnp.where(s0 == 2 * k, cols[fr * slots + s0] - base, span)
                item_b[item] = jnp.where(s0 + 1 < count, cols[fr * slots + s0 + 1] - base, span)
                return carry

            lax.fori_loop(0, here, each_pair, 0)
            return n + here

        total = lax.fori_loop(0, rows, each_row, total)
    for j in range(GROUP):
        item_row[total + j] = total_rows
        item_f[total + j] = 0
        item_buf[total + j] = 0
        item_a[total + j] = span
        item_b[total + j] = span
    groups = (total + GROUP - 1) // GROUP

    def arrive(g):
        for j in range(GROUP):
            @pl.when(g * GROUP + j < total)
            def _():
                copy_of(0, 0, 0, g * GROUP + j).wait()

    t[...] = jnp.zeros_like(t)
    lhs[total_rows] = jnp.zeros(lhs.shape[1:], lhs.dtype)
    if not first:
        inverse = 1.0 / stats[1]
        ratio = stats[1] / stats[0]
        for f in range(freqs):
            for c in range(2):
                scaled = field[c, f] * inverse[f : f + 1, :1]
                zb[c, f, :, : span * blk] = scaled.astype(jnp.bfloat16)
        zb[:, :, :, span * blk :] = jnp.zeros((2, freqs, sources, blk), jnp.bfloat16)
        acc[...] = jnp.zeros_like(acc)

        def forward(g, carry):
            arrive(g)
            for j in range(GROUP):
                i = g * GROUP + j
                f = item_f[i]
                za = zb[:, f, :, lanes(item_a[i])].reshape(2 * sources, blk)
                zc = zb[:, f, :, lanes(item_b[i])].reshape(2 * sources, blk)
                weights = buf[item_buf[i]].reshape(2, 2 * blk, blk)
                out = lax.dot_general(
                    jnp.concatenate([za, zc], axis=1),
                    jnp.concatenate([weights[0], weights[1]], axis=1),
                    (((1,), (1,)), ((), ())),
                    preferred_element_type=jnp.float32,
                )
                acc[item_row[i]] += out
            return carry

        lax.fori_loop(0, groups, forward, 0)

    for f in range(freqs):
        def finish(r, sums, f=f):
            fr = f * rows + r
            if first:
                real = start[0, f, :, lanes(r)]
                imag = start[1, f, :, lanes(r)]
                real16, imag16 = real, imag
                real, imag = real.astype(jnp.float32), imag.astype(jnp.float32)
            else:
                a = acc[fr]
                real = (
                    field[0, f, :, lanes(r + reach)] * inverse[f : f + 1, :]
                    + (a[:sources, :blk] - a[sources:, blk:])
                    - ratio[f : f + 1, :] * prev[0, f, :, lanes(r)]
                )
                imag = (
                    field[1, f, :, lanes(r + reach)] * inverse[f : f + 1, :]
                    + (a[:sources, blk:] + a[sources:, :blk])
                    - ratio[f : f + 1, :] * prev[1, f, :, lanes(r)]
                )
                p_out[0, f, :, lanes(r)] = real
                p_out[1, f, :, lanes(r)] = imag
                real16, imag16 = real.astype(jnp.bfloat16), imag.astype(jnp.bfloat16)
            t[0, f, :, lanes(r + reach)] = real
            t[1, f, :, lanes(r + reach)] = imag
            lhs[fr, :sources, :blk] = real16
            lhs[fr, :sources, blk:] = imag16
            lhs[fr, sources:, :blk] = imag16
            lhs[fr, sources:, blk:] = -real16
            squares = real * real + imag * imag
            return sums + jnp.sum(squares.reshape(sources // 8, 8, blk), axis=0)

        psq[f] = lax.fori_loop(0, rows, finish, jnp.zeros((8, blk), jnp.float32))

    def adjoint(g, carry):
        if first:
            arrive(g)
        for j in range(GROUP):
            i = g * GROUP + j
            f = item_f[i]
            weights = buf[item_buf[i]].reshape(2, 2 * blk, blk)
            out = jnp.dot(
                lhs[item_row[i]],
                jnp.concatenate([weights[0], weights[1]], axis=1),
                preferred_element_type=jnp.float32,
            )
            for index, half in ((item_a[i], out[:, :blk]), (item_b[i], out[:, blk:])):
                t[:, f, :, lanes(index)] += half.reshape(2, sources, blk)
        return carry

    lax.fori_loop(0, groups, adjoint, 0)


def operator_pass(counts, cols, blocks, start=None, field=None, stats=None, prev=None):
    freqs, rows, slots, _, blk, _ = blocks.shape
    first = start is not None
    sources = (start if first else prev).shape[2]
    reach = (slots - 1) // 2
    span = rows + 2 * reach
    pairs = (slots + 1) // 2
    items = freqs * rows * pairs
    dims = (freqs, rows, slots, blk, reach, sources)
    smem = pl.BlockSpec(memory_space=pltpu.SMEM)
    vmem = pl.BlockSpec(memory_space=pltpu.VMEM)
    hbm = pl.BlockSpec(memory_space=pl.ANY)
    t_shape = jax.ShapeDtypeStruct((2, freqs, sources, (span + 1) * blk), jnp.float32)
    psq_shape = jax.ShapeDtypeStruct((freqs, 8, blk), jnp.float32)
    listed = (items + GROUP,)
    scratch = [
        pltpu.VMEM((items, 2, 2, blk, blk), jnp.bfloat16),
        pltpu.VMEM((freqs * rows + 1, 2 * sources, 2 * blk), jnp.bfloat16),
        pltpu.SMEM(listed, jnp.int32),
        pltpu.SMEM(listed, jnp.int32),
        pltpu.SMEM(listed, jnp.int32),
        pltpu.SMEM(listed, jnp.int32),
        pltpu.SMEM(listed, jnp.int32),
        pltpu.SemaphoreType.DMA(((items + GROUP - 1) // GROUP,)),
    ]
    if first:
        args = (counts, cols, blocks, start)
        in_specs = [smem, smem, hbm, vmem]
        out_shape = (t_shape, psq_shape)
    else:
        args = (counts, cols, blocks, field, stats, prev)
        in_specs = [smem, smem, hbm, vmem, vmem, vmem]
        out_shape = (jax.ShapeDtypeStruct(prev.shape, jnp.float32), t_shape, psq_shape)
        scratch += [
            pltpu.VMEM((2, freqs, sources, (span + 1) * blk), jnp.bfloat16),
            pltpu.VMEM((freqs * rows + 1, 2 * sources, 2 * blk), jnp.float32),
        ]
    return pl.pallas_call(
        functools.partial(pass_kernel, first, dims),
        out_shape=out_shape,
        in_specs=in_specs,
        out_specs=tuple(vmem for _ in out_shape),
        scratch_shapes=scratch,
        compiler_params=pltpu.CompilerParams(vmem_limit_bytes=46 * 1024 * 1024),
        name="first_adjoint" if first else "forward_adjoint",
    )(*args)


def exchange_kernel(first, last, dims, *refs):
    freqs, rows, blk, reach, peers = dims
    t, psq, refs = refs[0], refs[1], refs[2:]
    if not first:
        before, stats_before, refs = refs[0], refs[1], refs[2:]
    q, stats, refs = refs[0], refs[1], refs[2:]
    (send_lo, send_hi, from_lo, from_hi, mine, theirs,
     rim_send, rim_recv, sum_send, sum_recv) = refs
    me = lax.axis_index("rcv")
    two = 2 * reach * blk
    rim = reach * blk
    span = (rows + 2 * reach) * blk
    has_lo = me > 0
    has_hi = me < peers - 1

    barrier = pltpu.get_barrier_semaphore()
    for d in range(1, peers):
        pl.semaphore_signal(
            barrier, inc=1, device_id={"rcv": lax.rem(me + d, peers)},
            device_id_type=pl.DeviceIdType.MESH,
        )
    send_lo[...] = t[:, :, :, :two].astype(jnp.bfloat16)
    send_hi[...] = t[:, :, :, span - two : span].astype(jnp.bfloat16)

    def to_row(parts):
        rows_of = [jnp.sum(part, axis=0, keepdims=True) for part in parts]
        rows_of.append(jnp.zeros((8 - len(parts), blk), jnp.float32))
        return jnp.concatenate(rows_of, axis=0)

    mine[0] = to_row([psq[f] for f in range(freqs)])
    pl.semaphore_wait(barrier, peers - 1)

    def sum_copy(k, d):
        return pltpu.make_async_remote_copy(
            src_ref=mine.at[k], dst_ref=theirs.at[k, d - 1],
            send_sem=sum_send.at[k, d - 1], recv_sem=sum_recv.at[k, d - 1],
            device_id={"rcv": lax.rem(me + d, peers)}, device_id_type=pl.DeviceIdType.MESH,
        )

    def lo_copy():
        return pltpu.make_async_remote_copy(
            src_ref=send_lo, dst_ref=from_hi, send_sem=rim_send.at[0], recv_sem=rim_recv.at[1],
            device_id={"rcv": lax.rem(me + peers - 1, peers)}, device_id_type=pl.DeviceIdType.MESH,
        )

    def hi_copy():
        return pltpu.make_async_remote_copy(
            src_ref=send_hi, dst_ref=from_lo, send_sem=rim_send.at[1], recv_sem=rim_recv.at[0],
            device_id={"rcv": lax.rem(me + 1, peers)}, device_id_type=pl.DeviceIdType.MESH,
        )

    for d in range(1, peers):
        sum_copy(0, d).start()

    @pl.when(has_lo)
    def _():
        lo_copy().start()

    @pl.when(has_hi)
    def _():
        hi_copy().start()

    @pl.when(jnp.logical_not(has_lo))
    def _():
        from_lo[...] = jnp.zeros_like(from_lo)

    @pl.when(jnp.logical_not(has_hi))
    def _():
        from_hi[...] = jnp.zeros_like(from_hi)

    def norm(k):
        total = mine[k]
        for d in range(1, peers):
            sum_copy(k, d).wait_recv()
        for d in range(1, peers):
            total += theirs[k, d - 1]
        value = jnp.sqrt(jnp.sum(total, axis=1, keepdims=True) + EPSILON)
        return jnp.broadcast_to(value, (8, blk))

    beta = norm(0)
    stats[0] = beta
    by_beta = 1.0 / beta
    if not first:
        pull = beta / stats_before[1]
    sums = [jnp.zeros((8, blk), jnp.float32) for _ in range(freqs)]

    def sweep(low, high, extra, offset):
        own = low >= rim and high <= span - rim
        if last and not own:
            return
        shift = rim if last else 0
        for f in range(freqs):
            for c in range(2):
                value = t[c, f, :, low:high]
                if extra is not None:
                    value += extra[c, f, :, offset : offset + high - low].astype(jnp.float32)
                value = value * by_beta[f : f + 1, :1]
                if not first:
                    value -= before[c, f, :, low:high] * pull[f : f + 1, :1]
                q[c, f, :, low - shift : high - shift] = value
                if own and not last:
                    squares = value * value
                    for j in range(0, high - low, blk):
                        part = squares[:, j : j + blk]
                        sums[f] = sums[f] + jnp.sum(part.reshape(-1, 8, blk), axis=0)

    if span > 2 * two:
        for low in range(two, span - two, rim):
            sweep(low, min(low + rim, span - two), None, 0)

    @pl.when(has_lo)
    def _():
        hi_like = pltpu.make_async_remote_copy(
            src_ref=send_hi, dst_ref=from_lo, send_sem=rim_send.at[1], recv_sem=rim_recv.at[0],
            device_id={"rcv": lax.rem(me + 1, peers)}, device_id_type=pl.DeviceIdType.MESH,
        )
        hi_like.wait_recv()

    sweep(rim, two, from_lo, rim)

    @pl.when(has_hi)
    def _():
        lo_copy().wait_recv()

    sweep(span - two, span - rim, from_hi, 0)
    if not last:
        mine[1] = to_row(sums)
        for d in range(1, peers):
            sum_copy(1, d).start()
        sweep(0, rim, from_lo, 0)
        sweep(span - rim, span, from_hi, rim)
        stats[1] = norm(1)
    for d in range(1, peers):
        sum_copy(0, d).wait_send()
        if not last:
            sum_copy(1, d).wait_send()

    @pl.when(has_lo)
    def _():
        lo_copy().wait_send()

    @pl.when(has_hi)
    def _():
        hi_copy().wait_send()


def exchange(t, psq, before, stats_before, dims, last):
    freqs, rows, blk, reach, peers = dims
    first = before is None
    sources = t.shape[2]
    vmem = pl.BlockSpec(memory_space=pltpu.VMEM)
    lanes = rows * blk if last else (rows + 2 * reach) * blk
    args = (t, psq) if first else (t, psq, before, stats_before)
    rim = pltpu.VMEM((2, freqs, sources, 2 * reach * blk), jnp.bfloat16)
    return pl.pallas_call(
        functools.partial(exchange_kernel, first, last, dims),
        out_shape=(
            jax.ShapeDtypeStruct((2, freqs, sources, lanes), jnp.float32),
            jax.ShapeDtypeStruct((2, 8, blk), jnp.float32),
        ),
        in_specs=[vmem] * len(args),
        out_specs=(vmem, vmem),
        scratch_shapes=[
            rim, rim, rim, rim,
            pltpu.VMEM((2, 8, blk), jnp.float32),
            pltpu.VMEM((2, peers - 1, 8, blk), jnp.float32),
            pltpu.SemaphoreType.DMA((2,)),
            pltpu.SemaphoreType.DMA((2,)),
            pltpu.SemaphoreType.DMA((2, peers - 1)),
            pltpu.SemaphoreType.DMA((2, peers - 1)),
        ],
        compiler_params=pltpu.CompilerParams(
            collective_id=0 if first else (2 if last else 1),
            has_side_effects=True,
            vmem_limit_bytes=16 * 1024 * 1024,
        ),
        name="exchange",
    )(*args)


def scatter_kernel(freq_groups, peers, send, recv, send_sem, recv_sem, own_sem):
    count = freq_groups * peers
    me = lax.axis_index("freq") * peers + lax.axis_index("rcv")

    def device(p):
        return (p // peers, lax.rem(p, peers))

    barrier = pltpu.get_barrier_semaphore()

    def greet(d, carry):
        pl.semaphore_signal(
            barrier, inc=1, device_id=device(lax.rem(me + d, count)),
            device_id_type=pl.DeviceIdType.MESH,
        )
        return carry

    lax.fori_loop(1, count, greet, 0)
    own = pltpu.make_async_copy(send.at[me], recv.at[me], own_sem)
    own.start()
    pl.semaphore_wait(barrier, count - 1)

    def copy_to(d, slot):
        to = lax.rem(me + d, count)
        return pltpu.make_async_remote_copy(
            src_ref=send.at[to], dst_ref=recv.at[slot],
            send_sem=send_sem.at[d - 1], recv_sem=recv_sem.at[d - 1],
            device_id=device(to), device_id_type=pl.DeviceIdType.MESH,
        )

    def begin(d, carry):
        copy_to(d, me).start()
        return carry

    def end(d, carry):
        copy = copy_to(d, lax.rem(me + count - d, count))
        copy.wait_send()
        copy.wait_recv()
        return carry

    lax.fori_loop(1, count, begin, 0)
    own.wait()
    lax.fori_loop(1, count, end, 0)


def scatter(spectrum, freq_groups, peers):
    vmem = pl.BlockSpec(memory_space=pltpu.VMEM)
    count = freq_groups * peers
    return pl.pallas_call(
        functools.partial(scatter_kernel, freq_groups, peers),
        out_shape=jax.ShapeDtypeStruct(spectrum.shape, spectrum.dtype),
        in_specs=[vmem],
        out_specs=vmem,
        scratch_shapes=[
            pltpu.SemaphoreType.DMA((count - 1,)),
            pltpu.SemaphoreType.DMA((count - 1,)),
            pltpu.SemaphoreType.DMA,
        ],
        compiler_params=pltpu.CompilerParams(
            collective_id=3, has_side_effects=True, vmem_limit_bytes=16 * 1024 * 1024
        ),
        name="scatter",
    )(spectrum)


def body(up_time, down_blocks, block_cols, block_counts):
    freq_groups = lax.axis_size("freq")
    receiver_groups = lax.axis_size("rcv")
    shot_count, time_steps, receivers = up_time.shape
    local_freqs, local_blocks, slot_count, _, block_size, _ = down_blocks.shape
    local_rows = receivers // receiver_groups
    reach_blocks = (slot_count - 1) // 2
    rim = reach_blocks * block_size
    fourier = fourier_table(time_steps, freq_groups * local_freqs)
    fourier = fourier.reshape(time_steps, -1).T
    spectrum = jnp.stack(
        [
            jnp.dot(fourier, up_time[s], preferred_element_type=jnp.float32).astype(jnp.bfloat16)
            for s in range(shot_count)
        ],
        axis=1,
    )
    spectrum = spectrum.reshape(
        2, freq_groups, local_freqs, shot_count, receiver_groups, local_rows
    ).transpose(1, 4, 0, 2, 3, 5)
    spectrum = spectrum.reshape(
        freq_groups * receiver_groups, 2 * local_freqs * shot_count, local_rows
    )
    received = scatter(spectrum, freq_groups, receiver_groups)
    received = received.reshape(-1, 2, local_freqs, shot_count, local_rows)
    right_side = received.transpose(1, 2, 0, 3, 4).reshape(2, local_freqs, -1, local_rows)
    counts = block_counts.reshape(-1)
    cols = block_cols.reshape(-1)
    ring = receiver_groups - 1
    up = [(i, i + 1) for i in range(ring)]
    down = [(i + 1, i) for i in range(ring)]

    def wide(value):
        return value[None, :, None, None]

    def stats_of(beta, alpha):
        rows = jnp.pad(jnp.stack([beta, alpha]), ((0, 0), (0, 8 - local_freqs)), constant_values=1.0)
        return jnp.broadcast_to(rows[:, :, None], (2, 8, block_size))

    def plain_exchange(t, psq, before, stats_before, last):
        lower = lax.ppermute(t[..., :rim], "rcv", down)
        upper = lax.ppermute(t[..., rim + local_rows : rim + local_rows + rim], "rcv", up)
        q = t[..., rim : rim + local_rows]
        q = q.at[..., :rim].add(upper)
        q = q.at[..., local_rows - rim :].add(lower)
        beta = jnp.sqrt(lax.psum(jnp.sum(psq, axis=(1, 2)), "rcv") + EPSILON)
        q = q / wide(beta)
        if before is not None:
            own = before[..., rim : rim + local_rows]
            q = q - wide(beta / stats_before[1, :local_freqs, 0]) * own
        if last:
            return q, stats_of(beta, beta)
        alpha = jnp.sqrt(lax.psum(jnp.sum(q * q, axis=(0, 2, 3)), "rcv") + EPSILON)
        below = lax.ppermute(q[..., local_rows - rim :], "rcv", up)
        above = lax.ppermute(q[..., :rim], "rcv", down)
        return jnp.concatenate([below, q, above], axis=-1), stats_of(beta, alpha)

    def step(t, psq, before, stats_before, last):
        if local_blocks < 2 * reach_blocks:
            return plain_exchange(t, psq, before, stats_before, last)
        dims = (local_freqs, local_blocks, block_size, reach_blocks, receiver_groups)
        return exchange(t, psq, before, stats_before, dims, last)

    t, psq = operator_pass(counts, cols, down_blocks, start=right_side)
    prev = right_side.astype(jnp.float32)
    q, stats = step(t, psq, None, None, False)
    fields, norms = [q], [stats]
    for iteration in range(ITERS):
        prev, t, psq = operator_pass(
            counts, cols, down_blocks, field=q, stats=stats, prev=prev
        )
        q, stats = step(t, psq, q, stats, iteration == ITERS - 1)
        fields.append(q)
        norms.append(stats)

    betas = [stats[0, :local_freqs, 0] for stats in norms]
    alphas = [stats[1, :local_freqs, 0] for stats in norms]
    phibar = betas[0]
    rhobar = alphas[0]
    weights = [jnp.zeros_like(phibar) for _ in range(ITERS)]
    direction = [1.0 / alphas[0]]
    for iteration in range(ITERS):
        beta = betas[iteration + 1]
        rho = jnp.sqrt(rhobar * rhobar + beta * beta)
        cosine = rhobar / rho
        sine = beta / rho
        phi = cosine * phibar
        phibar = sine * phibar
        for i, part in enumerate(direction):
            weights[i] = weights[i] + phi / rho * part
        if iteration == ITERS - 1:
            break
        alpha = alphas[iteration + 1]
        theta = sine * alpha
        rhobar = -cosine * alpha
        direction = [-theta / rho * part for part in direction] + [1.0 / alpha]
    x = sum(
        wide(weight) * field[..., rim : rim + local_rows]
        for weight, field in zip(weights, fields)
    )
    return (x, wide(phibar * cosine) * q)


def solution(mesh):
    return jax.shard_map(
        body,
        mesh=mesh,
        in_specs=(
            P(("freq", "rcv"), None, None),
            P("freq", "rcv", None, None, None, None),
            P("freq", "rcv", None),
            P("freq", "rcv"),
        ),
        out_specs=(P(None, "freq", None, "rcv"), P(None, "freq", None, "rcv")),
        check_vma=False,
    )
```
